256 devices in a mesh: rep: 64 (over y, z, x_hi), tp: 4 (over x_lo, core).
Axes of the slice: x: 4 (x_hi: 2, x_lo: 2; x = x_hi * 2 + x_lo), y: 4, z: 8, core: 2. Of those that a mesh axis runs over, the one named last changes fastest.
Arguments:
- hidden: bfloat16 [65536, 2560], P(('rep', 'tp')), may hold values from -6 to 6
- cotangent: bfloat16 [65536, 512], P('rep', 'tp'), may hold values from -6 to 6
- numerator: float32 [64, 2560, 512], P('rep', None, 'tp'), may hold values from -0.125 to 0.125
- push_weight: float32 [64], P('rep'), as said below
- moment_one: float32 [64, 2560, 512], P('rep', None, 'tp'), may hold values from -180 to 180
- moment_two: float32 [64, 2560, 512], P('rep', None, 'tp'), may hold values from 100 to 10000
- gossip_round: int32 [3], replicated, may hold values from 0 to 2, as said below
Outputs:
- numerator_out: float32 [64, 2560, 512], P('rep', None, 'tp')
- weight_out: float32 [64], P('rep')
- moment_one_out: float32 [64, 2560, 512], P('rep', None, 'tp')
- moment_two_out: float32 [64, 2560, 512], P('rep', None, 'tp')
- values: bfloat16 [65536, 512], P('rep', 'tp')
- grad_hidden: bfloat16 [65536, 2560], P(('rep', 'tp'))
The draws below stay inside these ranges and needn't reach their ends.
Inputs may be any that keep to these rules, and one draw needn't show every extreme that they name: `gossip_round`: each of the rounds 0, 1, 2 once. `push_weight`: positive.
All inputs are finite; a program needn't handle non-finite values.
Results may differ from the reference program's by a relative error of at most 0.015.
Values may be sent and summed in bfloat16 or wider, within the bound.
No kernel may reach another device: no remote copies, remote signals or barrier semaphores. Data moves between devices by JAX's collectives and lax.ppermute only.
A program may use at most 64 MiB of HBM per device.

```python
import math
import jax
import jax.numpy as jnp
from jax import lax

DW = 2560
KV = 512
TOK_DEV = 1024
TOKENS = 65536
N_REP = 64
N_TP = 4


def draw_push_weight(key, part):
    key = jax.random.fold_in(key, 11)
    expo = jax.random.uniform(key, (N_REP,), jnp.float32, -1.0, 1.0)
    return jnp.exp2(expo).astype(jnp.float32)


def draw_gossip_round(key, part):
    key = jax.random.fold_in(key, 23)
    return jax.random.permutation(key, jnp.arange(3, dtype=jnp.int32)).astype(jnp.int32)


def levels(stream_key, dims, shards, smallest, top_value):
    loudness = 1.0
    for dim, parts in shards:
        draws = jax.random.uniform(jax.random.fold_in(jax.random.fold_in(stream_key, 6), dim), (parts,), jnp.float32, smallest / len(shards), top_value / len(shards))
        loudness = loudness * jnp.repeat(jnp.exp(draws), dims[dim] // parts).reshape((-1,) + (1,) * (len(dims) - 1 - dim))
    return loudness


def scatter_about(own_key, extent, spread, bound, shards=(), held_as=jnp.bfloat16):
    factor_of = levels(own_key, extent, shards, -0.22, 0.18) if shards else 1.0
    values = jax.random.normal(own_key, extent, jnp.float32) * spread * factor_of
    return jnp.minimum(jnp.maximum(values, -bound), bound).astype(held_as)


def setup_inputs(seed: int = 0) -> dict:
    splits = jax.random.split(jax.random.key(seed), 8)
    hidden = scatter_about(splits[0], (TOKENS, DW), 1.0, 6.0, ((0, 256),))
    cotangent = scatter_about(splits[1], (TOKENS, KV), 1.0, 6.0, ((0, 64), (1, 4)))
    numerator = scatter_about(splits[2], (N_REP, DW, KV), DW ** -0.5, 0.125, ((0, 64), (2, 4)), jnp.float32)
    push_weight = draw_push_weight(jax.random.fold_in(splits[7], 71), 0)
    moment_one = scatter_about(splits[4], (N_REP, DW, KV), 30.0, 180.0, ((0, 64), (2, 4)), jnp.float32)
    moment_two = jnp.clip(jnp.exp(math.log(10000.0) - 4.6051702 * jax.random.uniform(splits[5], (N_REP, DW, KV), jnp.float32) ** levels(splits[5], (N_REP, DW, KV), ((0, 64), (2, 4)), -0.2, 0.2)), 100.0, 10000.0)
    gossip_round = draw_gossip_round(jax.random.fold_in(splits[7], 71), 0)
    return {"hidden": hidden, "cotangent": cotangent, "numerator": numerator, "push_weight": push_weight, "moment_one": moment_one, "moment_two": moment_two, "gossip_round": gossip_round}


def one_replica(items):
    hidden, cotangent, numerator, weight, moment_one, moment_two = items
    hid = hidden.astype(jnp.float32)
    scale = lax.rsqrt(lax.optimization_barrier(jnp.mean(hid * hid, axis=1, keepdims=True)) + 1e-06)
    normal = hid * scale
    normed = normal.astype(jnp.bfloat16)
    plain = numerator / weight
    debiased = plain.astype(jnp.bfloat16)
    values = jnp.dot(normed, debiased, preferred_element_type=jnp.float32).astype(jnp.bfloat16)
    grad = lax.dot_general(normed, cotangent, (((0,), (0,)), ((), ())), preferred_element_type=jnp.float32)
    block = KV // N_TP
    grad_normed = jnp.zeros(hid.shape, jnp.float32)
    for index in range(N_TP):
        cot_cols = cotangent[:, index * block:(index + 1) * block]
        deb_cols = debiased[:, index * block:(index + 1) * block]
        term = lax.dot_general(cot_cols, deb_cols, (((1,), (1,)), ((), ())), preferred_element_type=jnp.float32)
        term = lax.optimization_barrier(term.astype(jnp.bfloat16))
        grad_normed = grad_normed + term.astype(jnp.float32)
    inner = lax.optimization_barrier(jnp.mean(grad_normed * normal, axis=1, keepdims=True))
    grad_hidden = (scale * (grad_normed - normal * inner)).astype(jnp.bfloat16)
    first = 0.9 * moment_one + 0.1 * grad
    second = 0.95 * moment_two + 0.05 * grad * grad
    half = numerator - 0.001 * (first / (jnp.sqrt(second) + 1e-08) + 0.1 * plain)
    return (half, first, second, values, grad_hidden)

def reference(hidden, cotangent, numerator, push_weight, moment_one, moment_two, gossip_round):
    hid_all = hidden.reshape(N_REP, TOK_DEV, DW)
    cot_all = cotangent.reshape(N_REP, TOK_DEV, KV)
    half, first, second, values, grad_hidden = lax.map(one_replica, (hid_all, cot_all, numerator, push_weight, moment_one, moment_two))
    distance = jnp.left_shift(jnp.int32(1), gossip_round[0].astype(jnp.int32))
    numerator_out = 0.5 * (half + jnp.roll(half, distance, axis=0))
    weight_out = 0.5 * (push_weight + jnp.roll(push_weight, distance, axis=0))
    return (numerator_out, weight_out, first, second, values.reshape(TOKENS, KV), grad_hidden.reshape(TOKENS, DW))
```

```python
import functools

import jax
import jax.numpy as jnp
from jax import lax
from jax.experimental import pallas as pl
from jax.experimental.pallas import tpu as pltpu
from jax.sharding import PartitionSpec as P

F32 = jnp.float32
BF16 = jnp.bfloat16
ROWS = 256
FEATURES = 2560
COLS = 128
PIECES = 2
WIDTH = FEATURES // PIECES
STRIP = 16
VMEM = pl.BlockSpec(memory_space=pltpu.VMEM)
SMEM = pl.BlockSpec(memory_space=pltpu.SMEM)
ANY = pl.BlockSpec(memory_space=pl.ANY)
PARAMS = pltpu.CompilerParams(vmem_limit_bytes=48 * 1024 * 1024)


def swapped(value, flip):
    count = lax.axis_size("tp")
    return lax.ppermute(value, "tp", [(i, i ^ flip) for i in range(count)])


def pushed(value, distance):
    count = lax.axis_size("rep")
    return lax.ppermute(value, "rep", [(i, (i + distance) % count) for i in range(count)])


def rows_scale(ref, at):
    strip = ref[pl.ds(at, STRIP), :].astype(F32)
    return lax.rsqrt(jnp.sum(strip * strip, axis=1, keepdims=True) * (1.0 / FEATURES) + 1e-06)


def tdot(a, b):
    return lax.dot_general(a, b, (((0,), (0,)), ((), ())), preferred_element_type=F32)


def dott(a, b):
    return lax.dot_general(a, b, (((1,), (1,)), ((), ())), preferred_element_type=F32)


def scale_kernel(hid, scale):
    @pl.loop(0, ROWS, step=STRIP)
    def _(at):
        scale[pl.ds(at, STRIP), :] = jnp.broadcast_to(rows_scale(hid, at), (STRIP, COLS))


def grad_far_kernel(own, peer, scale_own, cot_far, cot_near, scale_peer, near, *rest):
    outs, far = rest[:-1], rest[-1]
    core = lax.rem(lax.axis_index("tp"), 2)
    mine = pl.multiple_of(core * ROWS, ROWS)
    other = pl.multiple_of((1 - core) * ROWS, ROWS)

    @pl.loop(0, ROWS, step=STRIP)
    def _(at):
        scale = jnp.broadcast_to(rows_scale(peer, at), (STRIP, COLS))
        scale_peer[pl.ds(at, STRIP), :] = scale
        far[pl.ds(ROWS + at, STRIP), :] = (cot_far[pl.ds(other + at, STRIP), :].astype(F32) * scale).astype(BF16)
        near[pl.ds(ROWS + at, STRIP), :] = (cot_near[pl.ds(other + at, STRIP), :].astype(F32) * scale).astype(BF16)

    own_scale = scale_own[...]
    far[:ROWS, :] = (cot_far[pl.ds(mine, ROWS), :].astype(F32) * own_scale).astype(BF16)
    near[:ROWS, :] = (cot_near[pl.ds(mine, ROWS), :].astype(F32) * own_scale).astype(BF16)
    for piece, out in enumerate(outs):
        span = pl.ds(piece * WIDTH, WIDTH)
        out[...] = (tdot(far[:ROWS, :], own[:, span]) + tdot(far[ROWS:, :], peer[:, span])).astype(BF16)


def moments_kernel(weight, own, peer, near, arrived, num, one, two, *rest):
    one_out, two_out, half, sent = rest[-4:]
    grad = tdot(near[:ROWS, :], own[...]) + tdot(near[ROWS:, :], peer[...]) + arrived[...].astype(F32)
    grad = grad.T
    first = 0.9 * one[...] + 0.1 * grad
    second = 0.95 * two[...] + 0.05 * grad * grad
    one_out[...] = first
    two_out[...] = second
    value = num[...] - 0.001 * (first / (jnp.sqrt(second) + 1e-08) + 0.1 * num[...] / weight[0])
    half[...] = value
    sent[...] = value.astype(BF16)


def mix_kernel(half, arrived, *rest):
    rest[-1][...] = 0.5 * (half[...] + arrived[...].astype(F32))


def values_kernel(own, peer, deb, deb_far, scale_own, scale_peer, near, far):
    core = lax.rem(lax.axis_index("tp"), 2)
    mine = pl.multiple_of(core * ROWS, ROWS)
    other = pl.multiple_of((1 - core) * ROWS, ROWS)
    for rows, scale, at in ((own, scale_own, mine), (peer, scale_peer, other)):
        for weights, out in ((deb, near), (deb_far, far)):
            product = jnp.dot(rows[...], weights[...], preferred_element_type=F32)
            out[pl.ds(at, ROWS), :] = (product * scale[...]).astype(BF16)


def peer_rows_kernel(cot_near, cot_far, deb, deb_far, out):
    core = lax.rem(lax.axis_index("tp"), 2)
    other = pl.multiple_of((1 - core) * ROWS, ROWS)
    near, far = cot_near[pl.ds(other, ROWS), :], cot_far[pl.ds(other, ROWS), :]
    for piece in range(4):
        span = pl.ds(piece * (FEATURES // 4), FEATURES // 4)
        out[:, span] = (dott(near, deb[span, :]) + dott(far, deb_far[span, :])).astype(BF16)


def hidden_kernel(own, scale_own, cot_near, cot_far, deb, deb_far, arrived, out, total):
    core = lax.rem(lax.axis_index("tp"), 2)
    mine = pl.multiple_of(core * ROWS, ROWS)
    near, far = cot_near[pl.ds(mine, ROWS), :], cot_far[pl.ds(mine, ROWS), :]
    for piece in range(4):
        span = pl.ds(piece * (FEATURES // 4), FEATURES // 4)
        total[:, span] = dott(near, deb[span, :]) + dott(far, deb_far[span, :]) + arrived[:, span].astype(F32)

    @pl.loop(0, ROWS, step=STRIP)
    def _(at):
        rows = pl.ds(at, STRIP)
        scale = scale_own[rows, :][:, :1]
        normal = own[rows, :].astype(F32) * scale
        grown = total[rows, :]
        inner = jnp.sum(grown * normal, axis=1, keepdims=True) * (1.0 / FEATURES)
        out[rows, :] = (scale * (grown - normal * inner)).astype(BF16)


def shape(*dims, kind=F32):
    return jax.ShapeDtypeStruct(dims, kind)


def step(distance, hidden, cotangent, numerator, push_weight, moment_one, moment_two):
    numerator, moment_one, moment_two = numerator[0], moment_one[0], moment_two[0]
    chip = lax.axis_index("tp") // 2
    cot_near = lax.dynamic_slice_in_dim(cotangent, chip * 2 * ROWS, 2 * ROWS, 0)
    cot_send = lax.dynamic_slice_in_dim(cotangent, (1 - chip) * 2 * ROWS, 2 * ROWS, 0)
    cot_far = swapped(cot_send, 2)
    peer = swapped(hidden, 1)
    deb = (numerator / push_weight[0]).astype(BF16)
    scale_own = pl.pallas_call(
        scale_kernel, out_shape=shape(ROWS, COLS), in_specs=[VMEM], out_specs=VMEM, compiler_params=PARAMS, name="row_scale"
    )(hidden)
    scale_peer, near, *parts = pl.pallas_call(
        grad_far_kernel,
        out_shape=[shape(ROWS, COLS), shape(2 * ROWS, COLS, kind=BF16)] + [shape(COLS, WIDTH, kind=BF16)] * PIECES,
        in_specs=[VMEM] * 5,
        out_specs=[VMEM] * (2 + PIECES),
        scratch_shapes=[pltpu.VMEM((2 * ROWS, COLS), BF16)],
        compiler_params=PARAMS,
        name="grad_far",
    )(hidden, peer, scale_own, cot_far, cot_near)
    parts = [swapped(part, 2) for part in parts]
    deb_far = swapped(deb, 2)
    whole = (None, None)
    halves, sent = [], []
    for piece in range(PIECES):
        block = pl.BlockSpec((WIDTH, COLS), lambda i, piece=piece: (piece, 0))
        columns = pl.BlockSpec((ROWS, WIDTH), lambda i, piece=piece: (0, piece))
        full = lambda *dims: pl.BlockSpec(dims, lambda i: (0,) * len(dims))
        extra = [] if piece == 0 else list(whole)
        one_out, two_out, half, out = pl.pallas_call(
            moments_kernel,
            grid=(1,),
            out_shape=[shape(FEATURES, COLS), shape(FEATURES, COLS), shape(WIDTH, COLS), shape(WIDTH, COLS, kind=BF16)],
            in_specs=[SMEM, columns, columns, full(2 * ROWS, COLS), full(COLS, WIDTH), block, block, block] + [ANY] * len(extra),
            out_specs=[block, block, full(WIDTH, COLS), full(WIDTH, COLS)],
            input_output_aliases={8: 0, 9: 1} if extra else {},
            compiler_params=PARAMS,
            name="moments",
        )(push_weight, hidden, peer, near, parts[piece], numerator, moment_one, moment_two, *extra)
        whole = (one_out, two_out)
        halves.append(half)
        sent.append(pushed(out, distance))
    weight_in = pushed(push_weight.astype(BF16), distance).astype(F32)
    weight_out = 0.5 * (push_weight + weight_in)
    for_peer = pl.pallas_call(
        peer_rows_kernel, out_shape=shape(ROWS, FEATURES, kind=BF16), in_specs=[VMEM] * 4, out_specs=VMEM, compiler_params=PARAMS, name="peer_rows"
    )(cot_near, cot_far, deb, deb_far)
    from_peer = swapped(for_peer, 1)
    value_near, value_far = pl.pallas_call(
        values_kernel,
        out_shape=[shape(2 * ROWS, COLS, kind=BF16)] * 2,
        in_specs=[VMEM] * 6,
        out_specs=[VMEM] * 2,
        compiler_params=PARAMS,
        name="values",
    )(hidden, peer, deb, deb_far, scale_own, scale_peer)
    value_in = swapped(value_far, 2)
    grad_hidden = pl.pallas_call(
        hidden_kernel,
        out_shape=shape(ROWS, FEATURES, kind=BF16),
        in_specs=[VMEM] * 7,
        out_specs=VMEM,
        scratch_shapes=[pltpu.VMEM((ROWS, FEATURES), F32)],
        compiler_params=PARAMS,
        name="grad_hidden",
    )(hidden, scale_own, cot_near, cot_far, deb, deb_far, from_peer)
    pair = jnp.where(chip == 0, jnp.concatenate([value_near, value_in]), jnp.concatenate([value_in, value_near]))
    mixed = None
    for piece in range(PIECES):
        block = pl.BlockSpec((WIDTH, COLS), lambda i, piece=piece: (piece, 0))
        full = lambda *dims: pl.BlockSpec(dims, lambda i: (0,) * len(dims))
        extra = [] if piece == 0 else [mixed]
        mixed = pl.pallas_call(
            mix_kernel,
            grid=(1,),
            out_shape=shape(FEATURES, COLS),
            in_specs=[full(WIDTH, COLS)] * 2 + [ANY] * len(extra),
            out_specs=block,
            input_output_aliases={2: 0} if extra else {},
            compiler_params=PARAMS,
            name="mix",
        )(halves[piece], sent[piece], *extra)
    return mixed[None], weight_out, whole[0][None], whole[1][None], pair, grad_hidden


def local(hidden, cotangent, numerator, push_weight, moment_one, moment_two, gossip_round):
    steps = [functools.partial(step, 2**level) for level in range(3)]
    return lax.switch(gossip_round[0], steps, hidden, cotangent, numerator, push_weight, moment_one, moment_two)


def solution(mesh):
    placed = (
        P(("rep", "tp"), None),
        P("rep", "tp"),
        P("rep", None, "tp"),
        P("rep"),
        P("rep", None, "tp"),
        P("rep", None, "tp"),
        P(),
    )
    return jax.shard_map(
        local,
        mesh=mesh,
        in_specs=placed,
        out_specs=(
            P("rep", None, "tp"),
            P("rep"),
            P("rep", None, "tp"),
            P("rep", None, "tp"),
            P("rep", "tp"),
            P(("rep", "tp"), None),
        ),
        check_vma=False,
    )
```

```python
import functools

import jax
import jax.numpy as jnp
from jax import lax
from jax.experimental import pallas as pl
from jax.experimental.pallas import tpu as pltpu
from jax.sharding import PartitionSpec as P

F32 = jnp.float32
BF16 = jnp.bfloat16
ROWS = 256
FEATURES = 2560
COLS = 128
GRADS = (1280, 1280)
WEIGHTS = (256, 1152, 1152)
STRIP = 16
VMEM = pl.BlockSpec(memory_space=pltpu.VMEM)
SMEM = pl.BlockSpec(memory_space=pltpu.SMEM)
ANY = pl.BlockSpec(memory_space=pl.ANY)
PARAMS = pltpu.CompilerParams(vmem_limit_bytes=48 * 1024 * 1024)


def spans(widths):
    starts = [sum(widths[:i]) for i in range(len(widths))]
    return list(zip(starts, widths))


def swapped(value, flip):
    count = lax.axis_size("tp")
    return lax.ppermute(value, "tp", [(i, i ^ flip) for i in range(count)])


def pushed(value, distance):
    count = lax.axis_size("rep")
    return lax.ppermute(value, "rep", [(i, (i + distance) % count) for i in range(count)])


def shape(*dims, kind=F32):
    return jax.ShapeDtypeStruct(dims, kind)


def like(array):
    return jax.ShapeDtypeStruct(array.shape, array.dtype)


def own_and_other():
    core = lax.rem(lax.axis_index("tp"), 2)
    return pl.multiple_of(core * ROWS, ROWS), pl.multiple_of((1 - core) * ROWS, ROWS)


def rows_scale(ref, at, count):
    rows = pl.ds(at, count)
    total = jnp.zeros((count, COLS), F32)
    for start in range(0, FEATURES, COLS):
        part = ref[rows, start:start + COLS].astype(F32)
        total = total + part * part
    scale = lax.rsqrt(jnp.sum(total, axis=1, keepdims=True) * (1.0 / FEATURES) + 1e-06)
    return jnp.broadcast_to(scale, (count, COLS))


def tdot(a, b):
    return lax.dot_general(a, b, (((0,), (0,)), ((), ())), preferred_element_type=F32)


def dott(a, b):
    return lax.dot_general(a, b, (((1,), (1,)), ((), ())), preferred_element_type=F32)


def prepare_kernel(weight, hid, num, _, scale, inverse, weight_rows, whole, *rest):
    outs, (hid_hold, num_hold, sems) = rest[:-3], rest[-3:]
    count = len(WEIGHTS)
    copies = []
    for i, (start, width) in enumerate(spans(WEIGHTS)):
        rows = pl.ds(start, width)
        copies.append(pltpu.make_async_copy(num.at[rows, :], num_hold.at[rows, :], sems.at[i]))
    for i in range(2):
        rows = pl.ds(i * 128, 128)
        copies.append(pltpu.make_async_copy(hid.at[rows, :], hid_hold.at[rows, :], sems.at[count + i]))
    for copy in copies:
        copy.start()
    value = jnp.full((STRIP, COLS), weight[0], F32)
    weight_rows[...] = value
    inverse[...] = 1.0 / value
    by = inverse[:1, :]
    for i, ((start, width), out) in enumerate(zip(spans(WEIGHTS), outs)):
        copies[i].wait()

        @pl.loop(0, width, step=128)
        def _(at, start=start, out=out):
            block = (num_hold[pl.ds(start + at, 128), :] * by).astype(BF16)
            out[pl.ds(at, 128), :] = block
            whole[pl.ds(start + at, 128), :] = block

    for i in range(2):
        copies[count + i].wait()

        @pl.loop(i * 128, i * 128 + 128, step=STRIP)
        def _(at):
            scale[pl.ds(at, STRIP), :] = rows_scale(hid_hold, at, STRIP)


def grad_far_kernel(own, peer, scale_own, cot_far, cot_near, scale_peer, near, *rest):
    outs, far = rest[:-1], rest[-1]
    mine, other = own_and_other()

    @pl.loop(0, ROWS, step=STRIP)
    def _(at):
        scale = rows_scale(peer, at, STRIP)
        scale_peer[pl.ds(at, STRIP), :] = scale
        far[pl.ds(ROWS + at, STRIP), :] = (cot_far[pl.ds(other + at, STRIP), :].astype(F32) * scale).astype(BF16)
        near[pl.ds(ROWS + at, STRIP), :] = (cot_near[pl.ds(other + at, STRIP), :].astype(F32) * scale).astype(BF16)
        scale = scale_own[pl.ds(at, STRIP), :]
        far[pl.ds(at, STRIP), :] = (cot_far[pl.ds(mine + at, STRIP), :].astype(F32) * scale).astype(BF16)
        near[pl.ds(at, STRIP), :] = (cot_near[pl.ds(mine + at, STRIP), :].astype(F32) * scale).astype(BF16)

    for (start, width), out in zip(spans(GRADS), outs):
        span = pl.ds(start, width)
        out[...] = (tdot(far[:ROWS, :], own[:, span]) + tdot(far[ROWS:, :], peer[:, span])).astype(BF16)


def moments_kernel(piece, carried, inverse, weight_rows, own, peer, near, arrived, num, one, two, *rest):
    first_out, second_out, half, sent = rest[carried:carried + 4]
    start, width = spans(GRADS)[piece]
    span = pl.ds(start, width)
    by = inverse[:1, :]
    grad = tdot(near[:ROWS, :], own[:, span]) + tdot(near[ROWS:, :], peer[:, span]) + arrived[...].astype(F32)
    for at in range(0, width, 128):
        rows, here = pl.ds(start + at, 128), pl.ds(at, 128)
        block = grad[:, at:at + 128].T
        first = 0.9 * one[rows, :] + 0.1 * block
        second = 0.95 * two[rows, :] + 0.05 * block * block
        first_out[here, :] = first
        second_out[here, :] = second
        value = num[rows, :]
        value = value - 0.001 * (first / (jnp.sqrt(second) + 1e-08) + 0.1 * (value * by))
        half[here, :] = value
        sent[here, :] = value.astype(BF16)
    if piece == 1:
        sent[width:, :] = weight_rows[...].astype(BF16)


def flush_kernel(first_a, first_b, second_a, second_b, half, arrived, first_out, second_out, mixed, sems):
    copies = []
    for pieces, out in (((first_a, first_b), first_out), ((second_a, second_b), second_out)):
        for (start, width), piece in zip(spans(GRADS), pieces):
            copies.append(pltpu.make_async_copy(piece, out.at[pl.ds(start, width), :], sems.at[len(copies)]))
    for copy in copies:
        copy.start()
    mixed[...] = 0.5 * (half[...] + arrived[...].astype(F32))
    for copy in copies:
        copy.wait()


def gate_kernel(far, *rest):
    rest[-1][...] = far[...]


def finish_kernel(weight_rows, half, arrived, mixed, value_near, value_in, _, out, weight_out, values, hold, sems):
    start, width = spans(GRADS)[1]
    copies = [pltpu.make_async_copy(mixed, out.at[pl.ds(0, start), :], sems.at[0])]
    copies[0].start()
    chip = lax.axis_index("tp") // 2
    for side, value in ((chip, value_near), (1 - chip, value_in)):
        rows = pl.ds(pl.multiple_of(side * 2 * ROWS, 2 * ROWS), 2 * ROWS)
        copies.append(pltpu.make_async_copy(value, values.at[rows, :], sems.at[len(copies)]))
        copies[-1].start()
    size = width // 2
    for at in range(0, width, size):
        here = pl.ds(at, size)
        hold[here, :] = 0.5 * (half[here, :] + arrived[here, :].astype(F32))
        copies.append(pltpu.make_async_copy(hold.at[here, :], out.at[pl.ds(start + at, size), :], sems.at[len(copies)]))
        copies[-1].start()
    mean = 0.5 * (weight_rows[...] + arrived[width:, :].astype(F32))
    weight_out[0] = jnp.max(mean)
    for copy in copies:
        copy.wait()


def values_kernel(own, peer, scale_own, scale_peer, deb, *rest):
    fars, (near, far_out, both) = rest[:-3], rest[-3:]
    mine, other = own_and_other()
    both[:, :COLS] = deb[...]
    for (start, width), far in zip(spans(WEIGHTS), fars):
        both[pl.ds(start, width), COLS:] = far[...]
    for rows, scale, at in ((own, scale_own, mine), (peer, scale_peer, other)):
        product = jnp.dot(rows[...], both[...], preferred_element_type=F32)
        near[pl.ds(at, ROWS), :] = (product[:, :COLS] * scale[...]).astype(BF16)
        far_out[pl.ds(at, ROWS), :] = (product[:, COLS:] * scale[...]).astype(BF16)


def hidden_kernel(own, scale_own, cot_near, cot_far, cross_near, cross_far, both, deb_peer, *rest):
    fars, (out, total, inner) = rest[:-3], rest[-3:]
    mine, _ = own_and_other()
    rows = jnp.concatenate([cot_near[pl.ds(mine, ROWS), :], cot_far[pl.ds(mine, ROWS), :], cross_near[...], cross_far[...]], axis=1)
    inner[...] = jnp.zeros_like(inner)
    for (start, width), far in zip(spans(WEIGHTS), fars):

        size = 384 if width % 384 == 0 else 256

        @pl.loop(0, width, step=size)
        def _(at, start=start, far=far, size=size):
            here = pl.ds(pl.multiple_of(at, COLS), size)
            span = pl.ds(pl.multiple_of(start + at, COLS), size)
            grown = dott(rows, jnp.concatenate([both[span, :], deb_peer[span, :], far[here, :]], axis=1))
            total[:, span] = grown
            part = grown * own[:, span].astype(F32)
            inner[...] += sum(part[:, i:i + COLS] for i in range(0, size, COLS))

    scale = scale_own[...]
    mean = jnp.sum(inner[...], axis=1, keepdims=True) * (1.0 / FEATURES)
    inner[...] = scale * (scale * (scale * mean))

    @pl.loop(0, FEATURES, step=256)
    def _(at):
        for part in range(2):
            span = pl.ds(pl.multiple_of(at + part * COLS, COLS), COLS)
            out[:, span] = (scale_own[...] * total[:, span] - own[:, span].astype(F32) * inner[...]).astype(BF16)


def run(kernel, name, outs, ins, operands, scratch=(), aliases=None):
    return pl.pallas_call(
        kernel,
        out_shape=[spec for spec, _ in outs],
        in_specs=ins,
        out_specs=[place for _, place in outs],
        scratch_shapes=list(scratch),
        input_output_aliases=aliases or {},
        compiler_params=PARAMS,
        cost_estimate=pl.CostEstimate(flops=1, bytes_accessed=1000000, transcendentals=0),
        name=name,
    )(*operands)


def step(
    distance, hidden, peer, numerator, moment_one, moment_two, cot_near, cot_far, near, cross_near, cross_far, scale_own, scale_peer, inverse, weight_rows, deb, far_first, *rest
):
    parts, debs = rest[:2], rest[2:]
    parts = [swapped(part, 2) for part in parts]
    deb_peer, first_peer = swapped(deb, 1), swapped(far_first, 1)
    made, sent, fars = [], [], [far_first]
    for piece, width in enumerate(GRADS):
        tokens = [made[0][2], first_peer] if piece == 1 else []
        result = run(
            functools.partial(moments_kernel, piece, 1 + len(tokens)),
            "moments",
            [(shape(width, COLS), VMEM)] * 3 + [(shape(width + piece * STRIP, COLS, kind=BF16), VMEM), (like(debs[piece]), ANY)],
            [VMEM] * 9 + [ANY] * (1 + len(tokens)),
            [inverse, weight_rows, hidden, peer, near, parts[piece], numerator, moment_one, moment_two, debs[piece], *tokens],
            aliases={9: 4},
        )
        made.append(result)
        sent.append(pushed(result[3], distance))
        fars.append(swapped(result[4], 2))
    one_out, two_out, mixed = run(
        flush_kernel,
        "flush",
        [(shape(FEATURES, COLS), ANY)] * 2 + [(shape(GRADS[0], COLS), VMEM)],
        [VMEM] * 6,
        [made[0][0], made[1][0], made[0][1], made[1][1], made[0][2], sent[0]],
        [pltpu.SemaphoreType.DMA((4,))],
    )
    (held,) = run(gate_kernel, "gate", [(like(fars[1]), VMEM)], [VMEM] + [ANY] * 2, [fars[1], mixed, deb_peer])
    fars_peer = [first_peer, *(swapped(far, 1) for far in (held, fars[2]))]
    value_near, value_far, both = run(
        values_kernel,
        "values",
        [(shape(2 * ROWS, COLS, kind=BF16), VMEM)] * 2 + [(shape(FEATURES, 2 * COLS, kind=BF16), VMEM)],
        [VMEM] * 8,
        [hidden, peer, scale_own, scale_peer, deb, *fars],
    )
    value_in = swapped(value_far, 2)
    (grad_hidden,) = run(
        hidden_kernel,
        "grad_hidden",
        [(shape(ROWS, FEATURES, kind=BF16), VMEM)],
        [VMEM] * 11,
        [hidden, scale_own, cot_near, cot_far, cross_near, cross_far, both, deb_peer, *fars_peer],
        [pltpu.VMEM((ROWS, FEATURES), F32), pltpu.VMEM((ROWS, COLS), F32)],
    )
    numerator_out, weight_out, values = run(
        finish_kernel,
        "finish",
        [(shape(FEATURES, COLS), ANY), (shape(1), SMEM), (shape(4 * ROWS, COLS, kind=BF16), ANY)],
        [VMEM] * 6 + [ANY],
        [weight_rows, made[1][2], sent[1], mixed, value_near, value_in, grad_hidden],
        [pltpu.VMEM((GRADS[1], COLS), F32), pltpu.SemaphoreType.DMA((6,))],
    )
    return numerator_out[None], weight_out, one_out[None], two_out[None], values, grad_hidden


def local(hidden, cotangent, numerator, push_weight, moment_one, moment_two, gossip_round):
    numerator, moment_one, moment_two = numerator[0], moment_one[0], moment_two[0]
    tp = lax.axis_index("tp")
    chip = tp // 2

    def cot_rows(start, count):
        return lax.dynamic_slice_in_dim(cotangent, start * ROWS, count * ROWS, 0)

    cot_send, cot_near = cot_rows((1 - chip) * 2, 2), cot_rows(chip * 2, 2)
    cot_far = swapped(cot_send, 2)
    peer = swapped(hidden, 1)
    cross_near = swapped(cot_rows(tp ^ 1, 1), 1)
    cross_far = swapped(cot_rows(tp ^ 3, 1), 3)
    scale_own, inverse, weight_rows, deb, *debs = run(
        prepare_kernel,
        "prepare",
        [(shape(ROWS, COLS), VMEM), (shape(STRIP, COLS), VMEM), (shape(STRIP, COLS), VMEM), (shape(FEATURES, COLS, kind=BF16), VMEM)]
        + [(shape(width, COLS, kind=BF16), VMEM) for width in WEIGHTS],
        [SMEM, ANY, ANY, ANY],
        [push_weight, hidden, numerator, cot_send],
        [pltpu.VMEM((ROWS, FEATURES), BF16), pltpu.VMEM((FEATURES, COLS), F32), pltpu.SemaphoreType.DMA((2 + len(WEIGHTS),))],
    )
    far_first = swapped(debs[0], 2)
    scale_peer, near, *parts = run(
        grad_far_kernel,
        "grad_far",
        [(shape(ROWS, COLS), VMEM), (shape(2 * ROWS, COLS, kind=BF16), VMEM)] + [(shape(COLS, width, kind=BF16), VMEM) for width in GRADS],
        [VMEM] * 5,
        [hidden, peer, scale_own, cot_far, cot_near],
        [pltpu.VMEM((2 * ROWS, COLS), BF16)],
    )
    steps = [functools.partial(step, 2**level) for level in range(3)]
    return lax.switch(
        gossip_round[0],
        steps,
        *(hidden, peer, numerator, moment_one, moment_two, cot_near, cot_far, near, cross_near, cross_far, scale_own, scale_peer, inverse, weight_rows, deb, far_first),
        *parts,
        *debs[1:],
    )


def solution(mesh):
    placed = (
        P(("rep", "tp"), None),
        P("rep", "tp"),
        P("rep", None, "tp"),
        P("rep"),
        P("rep", None, "tp"),
        P("rep", None, "tp"),
        P(),
    )
    return jax.shard_map(
        local,
        mesh=mesh,
        in_specs=placed,
        out_specs=(
            P("rep", None, "tp"),
            P("rep"),
            P("rep", None, "tp"),
            P("rep", None, "tp"),
            P("rep", "tp"),
            P(("rep", "tp"), None),
        ),
        check_vma=False,
    )
```

```python
import functools

import jax
import jax.numpy as jnp
from jax import lax
from jax.experimental import pallas as pl
from jax.experimental.pallas import tpu as pltpu
from jax.sharding import PartitionSpec as P

F32 = jnp.float32
BF16 = jnp.bfloat16
ROWS = 256
FEATURES = 2560
COLS = 128
GRADS = (1280, 1280)
WEIGHTS = (256, 1152, 1152)
HALF = 1280
STRIP = 16
BLOCK = 128
ORDER = (1, 2, 0)
VMEM = pl.BlockSpec(memory_space=pltpu.VMEM)
SMEM = pl.BlockSpec(memory_space=pltpu.SMEM)
ANY = pl.BlockSpec(memory_space=pl.ANY)
PARAMS = pltpu.CompilerParams(vmem_limit_bytes=48 * 1024 * 1024)


def spans(widths):
    starts = [sum(widths[:i]) for i in range(len(widths))]
    return list(zip(starts, widths))


def swapped(value, flip):
    count = lax.axis_size("tp")
    return lax.ppermute(value, "tp", [(i, i ^ flip) for i in range(count)])


def pushed(value, distance):
    count = lax.axis_size("rep")
    return lax.ppermute(value, "rep", [(i, (i + distance) % count) for i in range(count)])


def shape(*dims, kind=F32):
    return jax.ShapeDtypeStruct(dims, kind)


def like(array):
    return jax.ShapeDtypeStruct(array.shape, array.dtype)


def own_and_other():
    core = lax.rem(lax.axis_index("tp"), 2)
    return pl.multiple_of(core * ROWS, ROWS), pl.multiple_of((1 - core) * ROWS, ROWS)


def rows_scale(ref, at, count):
    rows = pl.ds(at, count)
    total = jnp.zeros((count, COLS), F32)
    for start in range(0, FEATURES, COLS):
        part = ref[rows, start:start + COLS].astype(F32)
        total = total + part * part
    scale = lax.rsqrt(jnp.sum(total, axis=1, keepdims=True) * (1.0 / FEATURES) + 1e-06)
    return jnp.broadcast_to(scale, (count, COLS))


def tdot(a, b):
    return lax.dot_general(a, b, (((0,), (0,)), ((), ())), preferred_element_type=F32)


def dott(a, b):
    return lax.dot_general(a, b, (((1,), (1,)), ((), ())), preferred_element_type=F32)


def split_kernel(cot, send, near, cross_near, cross_far, sems):
    tp = lax.axis_index("tp")
    chip = tp // 2
    starts = ((1 - chip) * 2, chip * 2, tp ^ 1, tp ^ 3)
    copies = []
    for i, (start, out) in enumerate(zip(starts, (send, near, cross_near, cross_far))):
        rows = pl.ds(pl.multiple_of(start * ROWS, ROWS), out.shape[0])
        copies.append(pltpu.make_async_copy(cot.at[rows, :], out, sems.at[i]))
        copies[-1].start()
    for copy in copies:
        copy.wait()


def prepare_kernel(weight, hid, num, _, scale, inverse, weight_rows, deb_a, deb_b, *rest):
    outs, (hid_hold, num_hold, sems) = rest[:-3], rest[-3:]
    count = len(WEIGHTS)
    copies = []
    for i, (start, width) in enumerate(spans(WEIGHTS)):
        rows = pl.ds(start, width)
        copies.append(pltpu.make_async_copy(num.at[rows, :], num_hold.at[rows, :], sems.at[i]))
    for i in range(2):
        rows = pl.ds(i * BLOCK, BLOCK)
        copies.append(pltpu.make_async_copy(hid.at[rows, :], hid_hold.at[rows, :], sems.at[count + i]))
    for copy in copies:
        copy.start()
    value = jnp.broadcast_to(weight[...], (STRIP, COLS))
    weight_rows[...] = value
    inverse[...] = 1.0 / value
    by = inverse[:1, :]
    for i, ((start, width), out) in enumerate(zip(spans(WEIGHTS), outs)):
        copies[i].wait()
        for at in range(0, width, BLOCK):
            block = (num_hold[start + at:start + at + BLOCK, :] * by).astype(BF16)
            out[at:at + BLOCK, :] = block
            place = start + at
            half, place = (deb_a, place) if place < HALF else (deb_b, place - HALF)
            half[place:place + BLOCK, :] = block

    for i in range(2):
        copies[count + i].wait()
        scale[i * BLOCK:i * BLOCK + BLOCK, :] = rows_scale(hid_hold, i * BLOCK, BLOCK)


def grad_far_kernel(own, peer, scale_own, cot_far, cot_near, scale_peer, near, *rest):
    outs, far = rest[:-1], rest[-1]
    mine, other = own_and_other()
    for at in range(0, ROWS, BLOCK):
        scale_peer[at:at + BLOCK, :] = rows_scale(peer, at, BLOCK)
    for base, start, scale in ((0, mine, scale_own), (ROWS, other, scale_peer)):
        for cot, out in ((cot_far, far), (cot_near, near)):
            out[base:base + ROWS, :] = (cot[pl.ds(start, ROWS), :].astype(F32) * scale[...]).astype(BF16)
    for (start, width), out in zip(spans(GRADS), outs):
        span = pl.ds(start, width)
        out[...] = (tdot(far[:ROWS, :], own[:, span]) + tdot(far[ROWS:, :], peer[:, span])).astype(BF16)


def moments_kernel(piece, carried, inverse, weight_rows, own, peer, near, arrived, num, one, two, *rest):
    first_out, second_out, half, sent = rest[carried:carried + 4]
    grads = rest[-1]
    start, width = spans(GRADS)[piece]
    span = pl.ds(start, width)
    by = inverse[:1, :]
    grads[...] = tdot(near[:ROWS, :], own[:, span]) + tdot(near[ROWS:, :], peer[:, span]) + arrived[...].astype(F32)

    @pl.loop(0, width, step=256)
    def _(at):
        for part in range(0, 256, 128):
            here = pl.ds(pl.multiple_of(at + part, 128), 128)
            rows = pl.ds(pl.multiple_of(start + at + part, 128), 128)
            block = grads[:, here].T
            first = 0.9 * one[rows, :] + 0.1 * block
            second = 0.95 * two[rows, :] + 0.05 * block * block
            first_out[here, :] = first
            second_out[here, :] = second
            value = num[rows, :]
            value = value - 0.001 * (first / (jnp.sqrt(second) + 1e-08) + 0.1 * (value * by))
            half[here, :] = value
            sent[here, :] = value.astype(BF16)

    if piece == 1:
        sent[width:, :] = weight_rows[...].astype(BF16)


def store_kernel(first_a, first_b, second_a, second_b, first_out, second_out, sems):
    copies = []
    for pieces, out in (((first_a, first_b), first_out), ((second_a, second_b), second_out)):
        for (start, width), piece in zip(spans(GRADS), pieces):
            copies.append(pltpu.make_async_copy(piece, out.at[pl.ds(start, width), :], sems.at[len(copies)]))
            copies[-1].start()
    for copy in copies:
        copy.wait()


def mix_kernel(half, arrived, deb, _, mixed, deb_out):
    deb_out[...] = deb[...]
    mixed[...] = 0.5 * (half[...] + arrived[...].astype(F32))


def finish_kernel(weight_rows, half, arrived, mixed, value_near, value_in, _, out, weight_out, values, hold, sems):
    start, width = spans(GRADS)[1]
    copies = [pltpu.make_async_copy(mixed, out.at[pl.ds(0, start), :], sems.at[0])]
    copies[0].start()
    chip = lax.axis_index("tp") // 2
    for side, value in ((chip, value_near), (1 - chip, value_in)):
        rows = pl.ds(pl.multiple_of(side * 2 * ROWS, 2 * ROWS), 2 * ROWS)
        copies.append(pltpu.make_async_copy(value, values.at[rows, :], sems.at[len(copies)]))
        copies[-1].start()
    size = width // 2
    for at in range(0, width, size):
        here = pl.ds(at, size)
        hold[here, :] = 0.5 * (half[here, :] + arrived[here, :].astype(F32))
        copies.append(pltpu.make_async_copy(hold.at[here, :], out.at[pl.ds(start + at, size), :], sems.at[len(copies)]))
        copies[-1].start()
    mean = 0.5 * (weight_rows[...] + arrived[width:, :].astype(F32))
    weight_out[0] = jnp.max(mean)
    for copy in copies:
        copy.wait()


def values_kernel(own, peer, scale_own, scale_peer, deb_a, deb_b, *rest):
    fars, (near, far_out) = rest[:-4], rest[-2:]
    mine, other = own_and_other()
    both = jnp.concatenate([jnp.concatenate([deb_a[...], deb_b[...]]), jnp.concatenate([far[...] for far in fars])], axis=1)
    for rows, scale, at in ((own, scale_own, mine), (peer, scale_peer, other)):
        product = jnp.dot(rows[...], both, preferred_element_type=F32)
        near[pl.ds(at, ROWS), :] = (product[:, :COLS] * scale[...]).astype(BF16)
        far_out[pl.ds(at, ROWS), :] = (product[:, COLS:] * scale[...]).astype(BF16)


def hidden_kernel(own, scale_own, cot_near, cot_far, cross_near, cross_far, *rest):
    out, total, weight = rest[-3:]
    count = len(WEIGHTS)
    groups = (rest[:2], rest[2:2 + count], rest[2 + count:4 + count], rest[4 + count:4 + 2 * count])
    mine, _ = own_and_other()
    rows = jnp.concatenate([cot_near[pl.ds(mine, ROWS), :], cot_far[pl.ds(mine, ROWS), :], cross_near[...], cross_far[...]], axis=1)
    columns = jnp.concatenate([jnp.concatenate([piece[...] for piece in group]) for group in groups], axis=1)
    total[...] = dott(rows, columns)
    inner = jnp.zeros((ROWS, COLS), F32)
    for at in range(0, FEATURES, COLS):
        inner = inner + total[:, at:at + COLS] * own[:, at:at + COLS].astype(F32)
    scale = scale_own[...]
    mean = jnp.sum(inner, axis=1, keepdims=True) * (1.0 / FEATURES)
    weight[...] = scale * (scale * (scale * mean))

    @pl.loop(0, FEATURES, step=512)
    def _(at):
        for part in range(0, 512, COLS):
            span = pl.ds(pl.multiple_of(at + part, COLS), COLS)
            out[:, span] = (scale_own[...] * total[:, span] - own[:, span].astype(F32) * weight[...]).astype(BF16)


def run(kernel, name, outs, ins, operands, scratch=(), aliases=None):
    return pl.pallas_call(
        kernel,
        out_shape=[spec for spec, _ in outs],
        in_specs=ins,
        out_specs=[place for _, place in outs],
        scratch_shapes=list(scratch),
        input_output_aliases=aliases or {},
        compiler_params=PARAMS,
        cost_estimate=pl.CostEstimate(flops=1, bytes_accessed=1000000, transcendentals=0),
        name=name,
    )(*operands)


def step(distance, hidden, peer, numerator, moment_one, moment_two, cots, near, scales, vectors, far_first, parts, halves, debs):
    parts = [swapped(part, 2) for part in parts]
    peer_a, first_peer = swapped(halves[0], 1), swapped(far_first, 1)
    made, sent, fars = [], [], [far_first]
    for piece, width in enumerate(GRADS):
        tokens = [made[0][2], first_peer] if piece == 1 else []
        result = run(
            functools.partial(moments_kernel, piece, 1 + len(tokens)),
            "moments",
            [(shape(width, COLS), VMEM)] * 3 + [(shape(width + piece * STRIP, COLS, kind=BF16), VMEM), (like(debs[piece]), ANY)],
            [VMEM] * 9 + [ANY] * (1 + len(tokens)),
            [*vectors, hidden, peer, near, parts[piece], numerator, moment_one, moment_two, debs[piece], *tokens],
            scratch=[pltpu.VMEM((COLS, width), F32)],
            aliases={9: 4},
        )
        made.append(result)
        sent.append(pushed(result[3], distance))
        fars.append(swapped(result[4], 2))
    one_out, two_out = run(
        store_kernel,
        "store",
        [(shape(FEATURES, COLS), ANY)] * 2,
        [VMEM] * 4,
        [made[0][0], made[1][0], made[0][1], made[1][1]],
        [pltpu.SemaphoreType.DMA((4,))],
    )
    mixed, held = run(
        mix_kernel,
        "mix",
        [(shape(GRADS[0], COLS), VMEM), (like(halves[1]), VMEM)],
        [VMEM] * 3 + [ANY],
        [made[0][2], sent[0], halves[1], one_out],
    )
    peer_b = swapped(held, 1)
    fars_peer = [first_peer, *(swapped(far, 1) for far in fars[1:])]
    value_near, value_far = run(
        values_kernel,
        "values",
        [(shape(2 * ROWS, COLS, kind=BF16), VMEM)] * 2,
        [VMEM] * (6 + len(fars)) + [ANY] * 2,
        [hidden, peer, *scales, *halves, *fars, peer_a, one_out],
    )
    value_in = swapped(value_far, 2)
    (grad_hidden,) = run(
        hidden_kernel,
        "grad_hidden",
        [(shape(ROWS, FEATURES, kind=BF16), VMEM)],
        [VMEM] * (10 + 2 * len(fars)),
        [hidden, scales[0], *cots, *halves, *fars, peer_a, peer_b, *fars_peer],
        [pltpu.VMEM((ROWS, FEATURES), F32), pltpu.VMEM((ROWS, COLS), F32)],
    )
    numerator_out, weight_out, values = run(
        finish_kernel,
        "finish",
        [(shape(FEATURES, COLS), ANY), (shape(1), SMEM), (shape(4 * ROWS, COLS, kind=BF16), ANY)],
        [VMEM] * 6 + [ANY],
        [vectors[1], made[1][2], sent[1], mixed, value_near, value_in, grad_hidden],
        [pltpu.VMEM((GRADS[1], COLS), F32), pltpu.SemaphoreType.DMA((6,))],
    )
    return numerator_out[None], weight_out, one_out[None], two_out[None], values, grad_hidden


def local(hidden, cotangent, numerator, push_weight, moment_one, moment_two, gossip_round):
    numerator, moment_one, moment_two = numerator[0], moment_one[0], moment_two[0]
    peer = swapped(hidden, 1)
    cot_send, cot_near, cross_near, cross_far = run(
        split_kernel,
        "split",
        [(shape(count * ROWS, COLS, kind=BF16), VMEM) for count in (2, 2, 1, 1)],
        [ANY],
        [cotangent],
        [pltpu.SemaphoreType.DMA((4,))],
    )
    cot_far = swapped(cot_send, 2)
    cots = [cot_near, cot_far, swapped(cross_near, 1), swapped(cross_far, 3)]
    scale_own, inverse, weight_rows, deb_a, deb_b, *debs = run(
        prepare_kernel,
        "prepare",
        [(shape(ROWS, COLS), VMEM), (shape(STRIP, COLS), VMEM), (shape(STRIP, COLS), VMEM)]
        + [(shape(width, COLS, kind=BF16), VMEM) for width in (HALF, FEATURES - HALF, *WEIGHTS)],
        [VMEM, ANY, ANY, ANY],
        [push_weight.reshape(1, 1), hidden, numerator, cot_send],
        [pltpu.VMEM((ROWS, FEATURES), BF16), pltpu.VMEM((FEATURES, COLS), F32), pltpu.SemaphoreType.DMA((2 + len(WEIGHTS),))],
    )
    far_first = swapped(debs[0], 2)
    scale_peer, near, *parts = run(
        grad_far_kernel,
        "grad_far",
        [(shape(ROWS, COLS), VMEM), (shape(2 * ROWS, COLS, kind=BF16), VMEM)] + [(shape(COLS, width, kind=BF16), VMEM) for width in GRADS],
        [VMEM] * 5,
        [hidden, peer, scale_own, cot_far, cot_near],
        [pltpu.VMEM((2 * ROWS, COLS), BF16)],
    )
    steps = [functools.partial(step, 2**level) for level in ORDER]
    scales, vectors, halves = [scale_own, scale_peer], [inverse, weight_rows], [deb_a, deb_b]
    return lax.switch(
        lax.rem(gossip_round[0] + 2, 3), steps, hidden, peer, numerator, moment_one, moment_two, cots, near, scales, vectors, far_first, parts, halves, debs[1:]
    )


def solution(mesh):
    placed = (
        P(("rep", "tp"), None),
        P("rep", "tp"),
        P("rep", None, "tp"),
        P("rep"),
        P("rep", None, "tp"),
        P("rep", None, "tp"),
        P(),
    )
    return jax.shard_map(
        local,
        mesh=mesh,
        in_specs=placed,
        out_specs=(
            P("rep", None, "tp"),
            P("rep"),
            P("rep", None, "tp"),
            P("rep", None, "tp"),
            P("rep", "tp"),
            P(("rep", "tp"), None),
        ),
        check_vma=False,
    )
```

```python
import functools

import jax
import jax.numpy as jnp
from jax import lax
from jax.experimental import pallas as pl
from jax.experimental.pallas import tpu as pltpu
from jax.sharding import PartitionSpec as P

F32 = jnp.float32
BF16 = jnp.bfloat16
ROWS = 256
FEATURES = 2560
COLS = 128
GRADS = (1280, 1280)
WEIGHTS = (1280, 1280)
HALF = 1280
STRIP = 16
BLOCK = 128
ORDER = (1, 2, 0)
VMEM = pl.BlockSpec(memory_space=pltpu.VMEM)
SMEM = pl.BlockSpec(memory_space=pltpu.SMEM)
ANY = pl.BlockSpec(memory_space=pl.ANY)
PARAMS = pltpu.CompilerParams(vmem_limit_bytes=48 * 1024 * 1024)


def spans(widths):
    starts = [sum(widths[:i]) for i in range(len(widths))]
    return list(zip(starts, widths))


def swapped(value, flip):
    count = lax.axis_size("tp")
    return lax.ppermute(value, "tp", [(i, i ^ flip) for i in range(count)])


def pushed(value, distance):
    count = lax.axis_size("rep")
    return lax.ppermute(value, "rep", [(i, (i + distance) % count) for i in range(count)])


def shape(*dims, kind=F32):
    return jax.ShapeDtypeStruct(dims, kind)


def like(array):
    return jax.ShapeDtypeStruct(array.shape, array.dtype)


def own_and_other():
    core = lax.rem(lax.axis_index("tp"), 2)
    return pl.multiple_of(core * ROWS, ROWS), pl.multiple_of((1 - core) * ROWS, ROWS)


def rows_scale(ref, at, count):
    rows = pl.ds(at, count)
    total = jnp.zeros((count, COLS), F32)
    for start in range(0, FEATURES, COLS):
        part = ref[rows, start:start + COLS].astype(F32)
        total = total + part * part
    scale = lax.rsqrt(jnp.sum(total, axis=1, keepdims=True) * (1.0 / FEATURES) + 1e-06)
    return jnp.broadcast_to(scale, (count, COLS))


def tdot(a, b):
    return lax.dot_general(a, b, (((0,), (0,)), ((), ())), preferred_element_type=F32)


def dott(a, b):
    return lax.dot_general(a, b, (((1,), (1,)), ((), ())), preferred_element_type=F32)


def split_kernel(cot, send, near, cross_near, cross_far, sems):
    tp = lax.axis_index("tp")
    chip = tp // 2
    starts = ((1 - chip) * 2, chip * 2, tp ^ 1, tp ^ 3)
    copies = []
    for i, (start, out) in enumerate(zip(starts, (send, near, cross_near, cross_far))):
        rows = pl.ds(pl.multiple_of(start * ROWS, ROWS), out.shape[0])
        copies.append(pltpu.make_async_copy(cot.at[rows, :], out, sems.at[i]))
        copies[-1].start()
    for copy in copies:
        copy.wait()


def scale_kernel(hid, _, scale):
    for at in range(0, ROWS, BLOCK):
        scale[at:at + BLOCK, :] = rows_scale(hid, at, BLOCK)


def prepare_kernel(weight, num, inverse, weight_rows, deb, *outs):
    value = jnp.full((STRIP, COLS), weight[0], F32)
    weight_rows[...] = value
    inverse[...] = 1.0 / value
    by = inverse[:1, :]
    for (start, width), out in zip(spans(WEIGHTS), outs):

        @pl.loop(0, width, step=BLOCK)
        def _(at, start=start, out=out):
            block = (num[pl.ds(start + at, BLOCK), :] * by).astype(BF16)
            out[pl.ds(at, BLOCK), :] = block
            deb[pl.ds(start + at, BLOCK), :] = block


def grad_far_kernel(own, peer, scale_own, cot_far, cot_near, scale_peer, near, *rest):
    outs, far = rest[:-1], rest[-1]
    mine, other = own_and_other()
    for at in range(0, ROWS, BLOCK):
        scale_peer[at:at + BLOCK, :] = rows_scale(peer, at, BLOCK)
    for base, start, scale in ((0, mine, scale_own), (ROWS, other, scale_peer)):
        for cot, out in ((cot_far, far), (cot_near, near)):
            out[base:base + ROWS, :] = (cot[pl.ds(start, ROWS), :].astype(F32) * scale[...]).astype(BF16)
    for (start, width), out in zip(spans(GRADS), outs):
        span = pl.ds(start, width)
        out[...] = (tdot(far[:ROWS, :], own[:, span]) + tdot(far[ROWS:, :], peer[:, span])).astype(BF16)


def moments_kernel(piece, carried, inverse, weight_rows, own, peer, near, arrived, num, one, two, *rest):
    first_out, second_out, half, sent = rest[carried:carried + 4]
    grads = rest[-1]
    start, width = spans(GRADS)[piece]
    span = pl.ds(start, width)
    by = inverse[:1, :]
    grads[...] = tdot(near[:ROWS, :], own[:, span]) + tdot(near[ROWS:, :], peer[:, span]) + arrived[...].astype(F32)

    @pl.loop(0, width, step=256)
    def _(at):
        for part in range(0, 256, 128):
            here = pl.ds(pl.multiple_of(at + part, 128), 128)
            rows = pl.ds(pl.multiple_of(start + at + part, 128), 128)
            block = grads[:, here].T
            first = 0.9 * one[rows, :] + 0.1 * block
            second = 0.95 * two[rows, :] + 0.05 * block * block
            first_out[here, :] = first
            second_out[here, :] = second
            value = num[rows, :]
            value = value - 0.001 * (first / (jnp.sqrt(second) + 1e-08) + 0.1 * (value * by))
            half[here, :] = value
            sent[here, :] = value.astype(BF16)

    sent[width:, :] = weight_rows[...].astype(BF16)


def store_kernel(first_a, first_b, second_a, second_b, first_out, second_out, sems):
    copies = []
    for pieces, out in (((first_a, first_b), first_out), ((second_a, second_b), second_out)):
        for (start, width), piece in zip(spans(GRADS), pieces):
            copies.append(pltpu.make_async_copy(piece, out.at[pl.ds(start, width), :], sems.at[len(copies)]))
            copies[-1].start()
    for copy in copies:
        copy.wait()


def mix_kernel(half, arrived, _, mixed):
    mixed[...] = 0.5 * (half[...] + arrived[:GRADS[0], :].astype(F32))


def finish_kernel(weight_rows, half, arrived, mixed, _, out, weight_out, hold, sems):
    start, width = spans(GRADS)[1]
    copies = [pltpu.make_async_copy(mixed, out.at[pl.ds(0, start), :], sems.at[0])]
    copies[0].start()
    size = width // 2
    for at in range(0, width, size):
        here = pl.ds(at, size)
        hold[here, :] = 0.5 * (half[here, :] + arrived[here, :].astype(F32))
        copies.append(pltpu.make_async_copy(hold.at[here, :], out.at[pl.ds(start + at, size), :], sems.at[len(copies)]))
        copies[-1].start()
    mean = 0.5 * (weight_rows[...] + arrived[width:, :].astype(F32))
    weight_out[0] = jnp.max(mean)
    for copy in copies:
        copy.wait()


def place_kernel(value_near, value_in, _, values, sems):
    chip = lax.axis_index("tp") // 2
    copies = []
    for side, value in ((chip, value_near), (1 - chip, value_in)):
        rows = pl.ds(pl.multiple_of(side * 2 * ROWS, 2 * ROWS), 2 * ROWS)
        copies.append(pltpu.make_async_copy(value, values.at[rows, :], sems.at[len(copies)]))
        copies[-1].start()
    for copy in copies:
        copy.wait()


def values_kernel(own, peer, scale_own, scale_peer, deb, *rest):
    fars, (near, far_out, far_a, far_b) = rest[:len(WEIGHTS)], rest[-4:]
    mine, other = own_and_other()
    far = jnp.concatenate([piece[...] for piece in fars])
    far_a[...] = far[:HALF]
    far_b[...] = far[HALF:]
    both = jnp.concatenate([deb[...], far], axis=1)
    for rows, scale, at in ((own, scale_own, mine), (peer, scale_peer, other)):
        product = jnp.dot(rows[...], both, preferred_element_type=F32)
        near[pl.ds(at, ROWS), :] = (product[:, :COLS] * scale[...]).astype(BF16)
        far_out[pl.ds(at, ROWS), :] = (product[:, COLS:] * scale[...]).astype(BF16)


def hidden_kernel(own, scale_own, cot_near, cot_far, cross_near, cross_far, *rest):
    out, total, weight = rest[-3:]
    count = len(WEIGHTS)
    groups = (rest[:1], rest[1:1 + count], rest[1 + count:2 + count], rest[2 + count:4 + count])
    mine, _ = own_and_other()
    rows = jnp.concatenate([cot_near[pl.ds(mine, ROWS), :], cot_far[pl.ds(mine, ROWS), :], cross_near[...], cross_far[...]], axis=1)
    columns = jnp.concatenate([jnp.concatenate([piece[...] for piece in group]) for group in groups], axis=1)
    total[...] = dott(rows, columns)
    inner = jnp.zeros((ROWS, COLS), F32)
    for at in range(0, FEATURES, COLS):
        inner = inner + total[:, at:at + COLS] * own[:, at:at + COLS].astype(F32)
    scale = scale_own[...]
    mean = jnp.sum(inner, axis=1, keepdims=True) * (1.0 / FEATURES)
    weight[...] = scale * (scale * (scale * mean))

    @pl.loop(0, FEATURES, step=512)
    def _(at):
        for part in range(0, 512, COLS):
            span = pl.ds(pl.multiple_of(at + part, COLS), COLS)
            out[:, span] = (scale_own[...] * total[:, span] - own[:, span].astype(F32) * weight[...]).astype(BF16)


def run(kernel, name, outs, ins, operands, scratch=(), aliases=None):
    return pl.pallas_call(
        kernel,
        out_shape=[spec for spec, _ in outs],
        in_specs=ins,
        out_specs=[place for _, place in outs],
        scratch_shapes=list(scratch),
        input_output_aliases=aliases or {},
        compiler_params=PARAMS,
        cost_estimate=pl.CostEstimate(flops=1, bytes_accessed=1000000, transcendentals=0),
        name=name,
    )(*operands)


def step(distance, push_weight, hidden, peer, numerator, moment_one, moment_two, cots, near, scales, parts):
    parts = [swapped(part, 2) for part in parts]
    inverse, weight_rows, deb, *debs = run(
        prepare_kernel,
        "prepare",
        [(shape(STRIP, COLS), VMEM)] * 2 + [(shape(width, COLS, kind=BF16), VMEM) for width in (FEATURES, *WEIGHTS)],
        [SMEM, VMEM],
        [push_weight, numerator],
    )
    vectors = [inverse, weight_rows]
    deb_peer = swapped(deb, 1)
    made, sent, fars = [], [], []
    for piece, width in enumerate(GRADS):
        tokens = [made[0][2]] if piece == 1 else []
        result = run(
            functools.partial(moments_kernel, piece, 1 + len(tokens)),
            "moments",
            [(shape(width, COLS), VMEM)] * 3 + [(shape(width + STRIP, COLS, kind=BF16), VMEM), (like(debs[piece]), ANY)],
            [VMEM] * 9 + [ANY] * (1 + len(tokens)),
            [*vectors, hidden, peer, near, parts[piece], numerator, moment_one, moment_two, debs[piece], *tokens],
            scratch=[pltpu.VMEM((COLS, width), F32)],
            aliases={9: 4},
        )
        made.append(result)
        sent.append(pushed(result[3], distance))
        fars.append(swapped(result[4], 2))
    one_out, two_out = run(
        store_kernel,
        "store",
        [(shape(FEATURES, COLS), ANY)] * 2,
        [VMEM] * 4,
        [made[0][0], made[1][0], made[0][1], made[1][1]],
        [pltpu.SemaphoreType.DMA((4,))],
    )
    (mixed,) = run(
        mix_kernel,
        "mix",
        [(shape(GRADS[0], COLS), VMEM)],
        [VMEM] * 2 + [ANY],
        [made[0][2], sent[0], one_out],
    )
    value_near, value_far, *far_halves = run(
        values_kernel,
        "values",
        [(shape(2 * ROWS, COLS, kind=BF16), VMEM)] * 2 + [(shape(rows, COLS, kind=BF16), VMEM) for rows in (HALF, FEATURES - HALF)],
        [VMEM] * (5 + len(fars)) + [ANY],
        [hidden, peer, *scales, deb, *fars, mixed],
    )
    value_in = swapped(value_far, 2)
    far_peer = [swapped(far, 1) for far in far_halves]
    (grad_hidden,) = run(
        hidden_kernel,
        "grad_hidden",
        [(shape(ROWS, FEATURES, kind=BF16), VMEM)],
        [VMEM] * (10 + len(fars)),
        [hidden, scales[0], *cots, deb, *fars, deb_peer, *far_peer],
        [pltpu.VMEM((ROWS, FEATURES), F32), pltpu.VMEM((ROWS, COLS), F32)],
    )

    def place(token):
        return run(
            place_kernel,
            "place",
            [(shape(4 * ROWS, COLS, kind=BF16), ANY)],
            [VMEM, VMEM, ANY],
            [value_near, value_in, token],
            [pltpu.SemaphoreType.DMA((2,))],
        )

    late = distance == 4
    if late:
        (values,) = place(grad_hidden)
    numerator_out, weight_out = run(
        finish_kernel,
        "finish",
        [(shape(FEATURES, COLS), ANY), (shape(1), SMEM)],
        [VMEM] * 4 + [ANY],
        [vectors[1], made[1][2], sent[1], mixed, values if late else grad_hidden],
        [pltpu.VMEM((GRADS[1], COLS), F32), pltpu.SemaphoreType.DMA((3,))],
    )
    if not late:
        (values,) = place(numerator_out)
    return numerator_out[None], weight_out, one_out[None], two_out[None], values, grad_hidden


def local(hidden, cotangent, numerator, push_weight, moment_one, moment_two, gossip_round):
    numerator, moment_one, moment_two = numerator[0], moment_one[0], moment_two[0]
    peer = swapped(hidden, 1)
    cot_send, cot_near, cross_near, cross_far = run(
        split_kernel,
        "split",
        [(shape(count * ROWS, COLS, kind=BF16), VMEM) for count in (2, 2, 1, 1)],
        [ANY],
        [cotangent],
        [pltpu.SemaphoreType.DMA((4,))],
    )
    cot_far = swapped(cot_send, 2)
    cots = [cot_near, cot_far, swapped(cross_near, 1), swapped(cross_far, 3)]
    (scale_own,) = run(scale_kernel, "row_scale", [(shape(ROWS, COLS), VMEM)], [VMEM, ANY], [hidden, cot_send])
    scale_peer, near, *parts = run(
        grad_far_kernel,
        "grad_far",
        [(shape(ROWS, COLS), VMEM), (shape(2 * ROWS, COLS, kind=BF16), VMEM)] + [(shape(COLS, width, kind=BF16), VMEM) for width in GRADS],
        [VMEM] * 5,
        [hidden, peer, scale_own, cot_far, cot_near],
        [pltpu.VMEM((2 * ROWS, COLS), BF16)],
    )
    steps = [functools.partial(step, 2**level) for level in ORDER]
    return lax.switch(
        lax.rem(gossip_round[0] + 2, 3),
        steps,
        *(push_weight, hidden, peer, numerator, moment_one, moment_two, cots, near, [scale_own, scale_peer], parts),
    )


def solution(mesh):
    placed = (
        P(("rep", "tp"), None),
        P("rep", "tp"),
        P("rep", None, "tp"),
        P("rep"),
        P("rep", None, "tp"),
        P("rep", None, "tp"),
        P(),
    )
    return jax.shard_map(
        local,
        mesh=mesh,
        in_specs=placed,
        out_specs=(
            P("rep", None, "tp"),
            P("rep"),
            P("rep", None, "tp"),
            P("rep", None, "tp"),
            P("rep", "tp"),
            P(("rep", "tp"), None),
        ),
        check_vma=False,
    )
```

```python
import functools

import jax
import jax.numpy as jnp
from jax import lax
from jax.experimental import pallas as pl
from jax.experimental.pallas import tpu as pltpu
from jax.sharding import PartitionSpec as P

F32 = jnp.float32
BF16 = jnp.bfloat16
ROWS = 256
FEATURES = 2560
COLS = 128
GRADS = (1280, 1280)
WEIGHTS = (1280, 1280)
HALF = 1280
STRIP = 16
BLOCK = 128
ORDER = (1, 2, 0)
VMEM = pl.BlockSpec(memory_space=pltpu.VMEM)
SMEM = pl.BlockSpec(memory_space=pltpu.SMEM)
ANY = pl.BlockSpec(memory_space=pl.ANY)
PARAMS = pltpu.CompilerParams(vmem_limit_bytes=48 * 1024 * 1024)


def spans(widths):
    starts = [sum(widths[:i]) for i in range(len(widths))]
    return list(zip(starts, widths))


def swapped(value, flip):
    count = lax.axis_size("tp")
    return lax.ppermute(value, "tp", [(i, i ^ flip) for i in range(count)])


def pushed(value, distance):
    count = lax.axis_size("rep")
    return lax.ppermute(value, "rep", [(i, (i + distance) % count) for i in range(count)])


def shape(*dims, kind=F32):
    return jax.ShapeDtypeStruct(dims, kind)


def like(array):
    return jax.ShapeDtypeStruct(array.shape, array.dtype)


def own_and_other():
    core = lax.rem(lax.axis_index("tp"), 2)
    return pl.multiple_of(core * ROWS, ROWS), pl.multiple_of((1 - core) * ROWS, ROWS)


def rows_scale(ref, at, count):
    rows = pl.ds(at, count)
    total = jnp.zeros((count, COLS), F32)
    for start in range(0, FEATURES, COLS):
        part = ref[rows, start:start + COLS].astype(F32)
        total = total + part * part
    scale = lax.rsqrt(jnp.sum(total, axis=1, keepdims=True) * (1.0 / FEATURES) + 1e-06)
    return jnp.broadcast_to(scale, (count, COLS))


def tdot(a, b):
    return lax.dot_general(a, b, (((0,), (0,)), ((), ())), preferred_element_type=F32)


def dott(a, b):
    return lax.dot_general(a, b, (((1,), (1,)), ((), ())), preferred_element_type=F32)


def split_kernel(cot, send, near, cross_near, cross_far, sems):
    tp = lax.axis_index("tp")
    chip = tp // 2
    starts = ((1 - chip) * 2, chip * 2, tp ^ 1, tp ^ 3)
    copies = []
    for i, (start, out) in enumerate(zip(starts, (send, near, cross_near, cross_far))):
        rows = pl.ds(pl.multiple_of(start * ROWS, ROWS), out.shape[0])
        copies.append(pltpu.make_async_copy(cot.at[rows, :], out, sems.at[i]))
        copies[-1].start()
    for copy in copies:
        copy.wait()


def scale_kernel(hid, _, scale):
    for at in range(0, ROWS, BLOCK):
        scale[at:at + BLOCK, :] = rows_scale(hid, at, BLOCK)


def prepare_kernel(weight, num, inverse, weight_rows, deb, *outs):
    value = jnp.full((STRIP, COLS), weight[0], F32)
    weight_rows[...] = value
    inverse[...] = 1.0 / value
    by = inverse[:1, :]
    for (start, width), out in zip(spans(WEIGHTS), outs):

        @pl.loop(0, width, step=BLOCK)
        def _(at, start=start, out=out):
            block = (num[pl.ds(start + at, BLOCK), :] * by).astype(BF16)
            out[pl.ds(at, BLOCK), :] = block
            deb[pl.ds(start + at, BLOCK), :] = block


def grad_far_kernel(own, peer, scale_own, cot_far, cot_near, scale_peer, near, *rest):
    outs, far = rest[:-1], rest[-1]
    mine, other = own_and_other()
    for at in range(0, ROWS, BLOCK):
        scale_peer[at:at + BLOCK, :] = rows_scale(peer, at, BLOCK)
    for base, start, scale in ((0, mine, scale_own), (ROWS, other, scale_peer)):
        for cot, out in ((cot_far, far), (cot_near, near)):
            out[base:base + ROWS, :] = (cot[pl.ds(start, ROWS), :].astype(F32) * scale[...]).astype(BF16)
    for (start, width), out in zip(spans(GRADS), outs):
        span = pl.ds(start, width)
        out[...] = (tdot(far[:ROWS, :], own[:, span]) + tdot(far[ROWS:, :], peer[:, span])).astype(BF16)


def moments_kernel(piece, carried, inverse, weight_rows, own, peer, near, arrived, num, one, two, *rest):
    first_out, second_out, half, sent = rest[carried:carried + 4]
    grads = rest[-1]
    start, width = spans(GRADS)[piece]
    span = pl.ds(start, width)
    by = inverse[:1, :]
    grads[...] = tdot(near[:ROWS, :], own[:, span]) + tdot(near[ROWS:, :], peer[:, span]) + arrived[...].astype(F32)

    @pl.loop(0, width, step=256)
    def _(at):
        for part in range(0, 256, 128):
            here = pl.ds(pl.multiple_of(at + part, 128), 128)
            rows = pl.ds(pl.multiple_of(start + at + part, 128), 128)
            block = grads[:, here].T
            first = 0.9 * one[rows, :] + 0.1 * block
            second = 0.95 * two[rows, :] + 0.05 * block * block
            first_out[here, :] = first
            second_out[here, :] = second
            value = num[rows, :]
            value = value - 0.001 * (first / (jnp.sqrt(second) + 1e-08) + 0.1 * (value * by))
            half[here, :] = value
            sent[here, :] = value.astype(BF16)

    sent[width:, :] = weight_rows[...].astype(BF16)


def store_kernel(first_a, first_b, second_a, second_b, first_out, second_out, sems):
    copies = []
    for pieces, out in (((first_a, first_b), first_out), ((second_a, second_b), second_out)):
        for (start, width), piece in zip(spans(GRADS), pieces):
            copies.append(pltpu.make_async_copy(piece, out.at[pl.ds(start, width), :], sems.at[len(copies)]))
            copies[-1].start()
    for copy in copies:
        copy.wait()


def mix_kernel(half, arrived, _, mixed):
    mixed[...] = 0.5 * (half[...] + arrived[:GRADS[0], :].astype(F32))


def place_copies(value_near, value_in, values, sems):
    chip = lax.axis_index("tp") // 2
    copies = []
    for side, value in ((chip, value_near), (1 - chip, value_in)):
        rows = pl.ds(pl.multiple_of(side * 2 * ROWS, 2 * ROWS), 2 * ROWS)
        copies.append(pltpu.make_async_copy(value, values.at[rows, :], sems.at[len(copies)]))
        copies[-1].start()
    return copies


def place_kernel(value_near, value_in, _, values, sems):
    for copy in place_copies(value_near, value_in, values, sems):
        copy.wait()


def finish_kernel(placing, weight_rows, half, arrived, mixed, _, *rest):
    near = ()
    if placing:
        near, rest = rest[:2], rest[2:]
    out, weight_out, *values, hold, sems = rest
    copies = place_copies(*near, *values, sems) if placing else []
    start, width = spans(GRADS)[1]
    copies.append(pltpu.make_async_copy(mixed, out.at[pl.ds(0, start), :], sems.at[len(copies)]))
    copies[-1].start()
    size = width // 2
    for at in range(0, width, size):
        here = pl.ds(at, size)
        hold[here, :] = 0.5 * (half[here, :] + arrived[here, :].astype(F32))
        copies.append(pltpu.make_async_copy(hold.at[here, :], out.at[pl.ds(start + at, size), :], sems.at[len(copies)]))
        copies[-1].start()
    mean = 0.5 * (weight_rows[...] + arrived[width:, :].astype(F32))
    weight_out[0] = jnp.max(mean)
    for copy in copies:
        copy.wait()


def values_kernel(tokens, own, peer, scale_own, scale_peer, deb, *rest):
    fars = rest[:len(WEIGHTS)]
    near, far_out, far_a, far_b = rest[len(WEIGHTS) + tokens:len(WEIGHTS) + tokens + 4]
    mine, other = own_and_other()
    far = jnp.concatenate([piece[...] for piece in fars])
    far_a[...] = far[:HALF]
    far_b[...] = far[HALF:]
    both = jnp.concatenate([deb[...], far], axis=1)
    for rows, scale, at in ((own, scale_own, mine), (peer, scale_peer, other)):
        product = jnp.dot(rows[...], both, preferred_element_type=F32)
        near[pl.ds(at, ROWS), :] = (product[:, :COLS] * scale[...]).astype(BF16)
        far_out[pl.ds(at, ROWS), :] = (product[:, COLS:] * scale[...]).astype(BF16)


def hidden_kernel(own, scale_own, cot_near, cot_far, cross_near, cross_far, *rest):
    out, total, weight, hold, sems = rest[-5:]
    count = len(WEIGHTS)
    groups = (rest[:1], rest[1:1 + count], rest[1 + count:2 + count], rest[2 + count:4 + count])
    mine, _ = own_and_other()
    rows = jnp.concatenate([cot_near[pl.ds(mine, ROWS), :], cot_far[pl.ds(mine, ROWS), :], cross_near[...], cross_far[...]], axis=1)
    columns = jnp.concatenate([jnp.concatenate([piece[...] for piece in group]) for group in groups], axis=1)
    total[...] = dott(rows, columns)
    inner = jnp.zeros((ROWS, COLS), F32)
    for at in range(0, FEATURES, COLS):
        inner = inner + total[:, at:at + COLS] * own[:, at:at + COLS].astype(F32)
    scale = scale_own[...]
    mean = jnp.sum(inner, axis=1, keepdims=True) * (1.0 / FEATURES)
    weight[...] = scale * (scale * (scale * mean))

    copies = []
    for at in range(0, FEATURES, 640):
        chunk = pl.ds(at, 640)
        copies.append(pltpu.make_async_copy(hold.at[:, chunk], out.at[:, chunk], sems.at[len(copies)]))

    @pl.loop(0, len(copies))
    def _(i):
        for part in range(0, 640, COLS):
            span = pl.ds(pl.multiple_of(i * 640 + part, COLS), COLS)
            hold[:, span] = (scale_own[...] * total[:, span] - own[:, span].astype(F32) * weight[...]).astype(BF16)
        chunk = pl.ds(pl.multiple_of(i * 640, COLS), 640)
        pltpu.make_async_copy(hold.at[:, chunk], out.at[:, chunk], sems.at[i]).start()

    for copy in copies:
        copy.wait()


def run(kernel, name, outs, ins, operands, scratch=(), aliases=None):
    return pl.pallas_call(
        kernel,
        out_shape=[spec for spec, _ in outs],
        in_specs=ins,
        out_specs=[place for _, place in outs],
        scratch_shapes=list(scratch),
        input_output_aliases=aliases or {},
        compiler_params=PARAMS,
        cost_estimate=pl.CostEstimate(flops=1, bytes_accessed=1000000, transcendentals=0),
        name=name,
    )(*operands)


def step(distance, push_weight, hidden, peer, numerator, moment_one, moment_two, cots, near, scales, parts):
    parts = [swapped(part, 2) for part in parts]
    inverse, weight_rows, deb, *debs = run(
        prepare_kernel,
        "prepare",
        [(shape(STRIP, COLS), VMEM)] * 2 + [(shape(width, COLS, kind=BF16), VMEM) for width in (FEATURES, *WEIGHTS)],
        [SMEM, VMEM],
        [push_weight, numerator],
    )
    vectors = [inverse, weight_rows]
    deb_peer = swapped(deb, 1)
    made, sent, fars = [], [], []
    for piece, width in enumerate(GRADS):
        tokens = [made[0][2]] if piece == 1 else []
        result = run(
            functools.partial(moments_kernel, piece, 1 + len(tokens)),
            "moments",
            [(shape(width, COLS), VMEM)] * 3 + [(shape(width + STRIP, COLS, kind=BF16), VMEM), (like(debs[piece]), ANY)],
            [VMEM] * 9 + [ANY] * (1 + len(tokens)),
            [*vectors, hidden, peer, near, parts[piece], numerator, moment_one, moment_two, debs[piece], *tokens],
            scratch=[pltpu.VMEM((COLS, width), F32)],
            aliases={9: 4},
        )
        made.append(result)
        sent.append(pushed(result[3], distance))
        fars.append(swapped(result[4], 2))
    one_out, two_out = run(
        store_kernel,
        "store",
        [(shape(FEATURES, COLS), ANY)] * 2,
        [VMEM] * 4,
        [made[0][0], made[1][0], made[0][1], made[1][1]],
        [pltpu.SemaphoreType.DMA((4,))],
    )
    (mixed,) = run(
        mix_kernel,
        "mix",
        [(shape(GRADS[0], COLS), VMEM)],
        [VMEM] * 2 + [ANY],
        [made[0][2], sent[0], one_out],
    )
    tokens = [mixed, deb_peer] if distance == 4 else [mixed]
    value_near, value_far, *far_halves = run(
        functools.partial(values_kernel, len(tokens)),
        "values",
        [(shape(2 * ROWS, COLS, kind=BF16), VMEM)] * 2 + [(shape(rows, COLS, kind=BF16), VMEM) for rows in (HALF, FEATURES - HALF)],
        [VMEM] * (5 + len(fars)) + [ANY] * len(tokens),
        [hidden, peer, *scales, deb, *fars, *tokens],
    )
    value_in = swapped(value_far, 2)
    far_peer = [swapped(far, 1) for far in far_halves]
    (grad_hidden,) = run(
        hidden_kernel,
        "grad_hidden",
        [(shape(ROWS, FEATURES, kind=BF16), ANY)],
        [VMEM] * (10 + len(fars)),
        [hidden, scales[0], *cots, deb, *fars, deb_peer, *far_peer],
        [pltpu.VMEM((ROWS, FEATURES), F32), pltpu.VMEM((ROWS, COLS), F32), pltpu.VMEM((ROWS, FEATURES), BF16), pltpu.SemaphoreType.DMA((4,))],
    )

    late = distance == 4
    values_out = (shape(4 * ROWS, COLS, kind=BF16), ANY)
    if late:
        (values,) = run(
            place_kernel, "place", [values_out], [VMEM, VMEM, ANY], [value_near, value_in, grad_hidden], [pltpu.SemaphoreType.DMA((2,))]
        )
    numerator_out, weight_out, *rest = run(
        functools.partial(finish_kernel, not late),
        "finish",
        [(shape(FEATURES, COLS), ANY), (shape(1), SMEM)] + ([] if late else [values_out]),
        [VMEM] * 4 + [ANY] + ([] if late else [VMEM] * 2),
        [vectors[1], made[1][2], sent[1], mixed] + ([values] if late else [grad_hidden, value_near, value_in]),
        [pltpu.VMEM((GRADS[1], COLS), F32), pltpu.SemaphoreType.DMA((3 if late else 5,))],
    )
    if not late:
        (values,) = rest
    return numerator_out[None], weight_out, one_out[None], two_out[None], values, grad_hidden


def local(hidden, cotangent, numerator, push_weight, moment_one, moment_two, gossip_round):
    numerator, moment_one, moment_two = numerator[0], moment_one[0], moment_two[0]
    peer = swapped(hidden, 1)
    cot_send, cot_near, cross_near, cross_far = run(
        split_kernel,
        "split",
        [(shape(count * ROWS, COLS, kind=BF16), VMEM) for count in (2, 2, 1, 1)],
        [ANY],
        [cotangent],
        [pltpu.SemaphoreType.DMA((4,))],
    )
    cot_far = swapped(cot_send, 2)
    cots = [cot_near, cot_far, swapped(cross_near, 1), swapped(cross_far, 3)]
    (scale_own,) = run(scale_kernel, "row_scale", [(shape(ROWS, COLS), VMEM)], [VMEM, ANY], [hidden, cot_send])
    scale_peer, near, *parts = run(
        grad_far_kernel,
        "grad_far",
        [(shape(ROWS, COLS), VMEM), (shape(2 * ROWS, COLS, kind=BF16), VMEM)] + [(shape(COLS, width, kind=BF16), VMEM) for width in GRADS],
        [VMEM] * 5,
        [hidden, peer, scale_own, cot_far, cot_near],
        [pltpu.VMEM((2 * ROWS, COLS), BF16)],
    )
    steps = [functools.partial(step, 2**level) for level in ORDER]
    return lax.switch(
        lax.rem(gossip_round[0] + 2, 3),
        steps,
        *(push_weight, hidden, peer, numerator, moment_one, moment_two, cots, near, [scale_own, scale_peer], parts),
    )


def solution(mesh):
    placed = (
        P(("rep", "tp"), None),
        P("rep", "tp"),
        P("rep", None, "tp"),
        P("rep"),
        P("rep", None, "tp"),
        P("rep", None, "tp"),
        P(),
    )
    return jax.shard_map(
        local,
        mesh=mesh,
        in_specs=placed,
        out_specs=(
            P("rep", None, "tp"),
            P("rep"),
            P("rep", None, "tp"),
            P("rep", None, "tp"),
            P("rep", "tp"),
            P(("rep", "tp"), None),
        ),
        check_vma=False,
    )
```
